512 devices in a mesh: seq: 128 (over x, y_lo, z, core), tp: 4 (over y_hi).
Axes of the slice: x: 4, y: 8 (y_hi: 4, y_lo: 2; y = y_hi * 2 + y_lo), z: 8, core: 2. Of those that a mesh axis runs over, the one named last changes fastest.
Arguments:
- queries: bfloat16 [16384, 5120], P('seq', 'tp'), may hold values from -72 to 72
- keys: bfloat16 [16384, 5120], P('seq', 'tp'), may hold values from -72 to 72
- values: bfloat16 [16384, 5120], P('seq', 'tp'), may hold values from -6 to 6
- query_gain: float32 [5120], P('tp'), may hold values from 0.1 to 1.9
- key_gain: float32 [5120], P('tp'), may hold values from 0.1 to 1.9
Outputs:
- mixed: bfloat16 [16384, 5120], P('seq', 'tp')
The draws below stay inside these ranges and needn't reach their ends.
All inputs are finite; a program needn't handle non-finite values.
Results may differ from the reference program's by a relative error of at most 0.0077.
Values may be sent and summed in bfloat16 or wider, within the bound.
No kernel may reach another device: no remote copies, remote signals or barrier semaphores. Data moves between devices by JAX's collectives and lax.ppermute only.
A program may use at most 64 MiB of HBM per device.

```python
import math
import jax
import jax.numpy as jnp
from jax import lax

D = 5120
HEADS = 40
HEAD_DIM = 128
FRAME_POS = 1024
FRAMES = 16
TOKENS = 16384


def scaled(key, base, power):
    key_row, key_col = jax.random.split(key)
    row_scale = jnp.exp(jax.random.uniform(key_row, (TOKENS, 1), jnp.float32, 0.0, math.log(3.2)))
    col_scale = jnp.exp(jax.random.uniform(key_col, (1, D), jnp.float32, 0.0, math.log(3.2)))
    ramp = jnp.exp(power * math.log(3.0) * jnp.arange(D, dtype=jnp.float32)[None, :] / D)
    return base * row_scale * col_scale * ramp


def draw_queries(key, part):
    key = jax.random.fold_in(key, 1)
    key_base, key_scale = jax.random.split(key, 2)
    base = jnp.clip(jax.random.normal(key_base, (TOKENS, D), jnp.float32), -4.0, 4.0)
    field = scaled(key_scale, base, 0.5)
    return field.astype(jnp.bfloat16)


def draw_keys(key, part):
    key = jax.random.fold_in(key, 2)
    key_base, key_scale = jax.random.split(key, 2)
    base = jnp.clip(jax.random.normal(key_base, (TOKENS, D), jnp.float32), -4.0, 4.0)
    field = scaled(key_scale, base, 0.5)
    return field.astype(jnp.bfloat16)


def level_of(key, shape, shards, low, top_value):
    level = 1.0
    for dim, blocks in shards:
        heights = jax.random.uniform(jax.random.fold_in(jax.random.fold_in(key, 6), dim), (blocks,), jnp.float32, low / len(shards), top_value / len(shards))
        level = level * jnp.repeat(jnp.exp(heights), shape[dim] // blocks).reshape((-1,) + (1,) * (len(shape) - 1 - dim))
    return level


def normal_values(own_key, shape, deviation, bound, cuts=(), kind=jnp.bfloat16):
    drawn = deviation * jax.random.normal(own_key, shape, jnp.float32)
    if cuts:
        drawn = drawn * level_of(own_key, shape, cuts, -0.22, 0.18)
    return jnp.clip(drawn, -bound, bound).astype(kind)


def setup_inputs(seed: int = 0) -> dict:
    key_list = jax.random.split(jax.random.key(seed), 6)
    queries = draw_queries(jax.random.fold_in(key_list[5], 71), 0)
    keys = draw_keys(jax.random.fold_in(key_list[5], 71), 0)
    values = normal_values(key_list[2], (TOKENS, D), 1.0, 6.0, ((0, 128), (1, 4)))
    query_gain = jnp.clip(1.0 + 0.18 * jax.random.normal(key_list[3], (D,), jnp.float32), 0.1, 1.9)
    key_gain = jnp.clip(1.0 + 0.18 * jax.random.normal(key_list[4], (D,), jnp.float32), 0.1, 1.9)
    return dict(queries=queries, keys=keys, values=values, query_gain=query_gain, key_gain=key_gain)


def norm_rows(block_in, gain_vec):
    widened = block_in.astype(jnp.float32)
    mean_sq = lax.optimization_barrier(jnp.mean(widened * widened, axis=-1, keepdims=True))
    return (widened * lax.rsqrt(mean_sq + 1e-06) * gain_vec.astype(jnp.float32)).astype(jnp.bfloat16)

def attend(query_blk, key_blk, value_blk):
    scores = jnp.einsum('...qhe,...khe->...hqk', query_blk.astype(jnp.float32), key_blk.astype(jnp.float32)) / math.sqrt(query_blk.shape[-1])
    top_score = lax.optimization_barrier(jnp.max(scores, axis=-1, keepdims=True))
    raised = jnp.exp(scores - top_score)
    weights = (raised / lax.optimization_barrier(jnp.sum(raised, axis=-1, keepdims=True))).astype(jnp.bfloat16)
    weights = lax.optimization_barrier(weights).astype(jnp.float32)
    return jnp.einsum('...hqk,...khe->...qhe', weights, value_blk.astype(jnp.float32))

def reference(queries, keys, values, query_gain, key_gain):
    q_norm = lax.map(lambda block_in: norm_rows(block_in, query_gain), queries.reshape(FRAMES, FRAME_POS, D))
    k_norm = lax.map(lambda block_in: norm_rows(block_in, key_gain), keys.reshape(FRAMES, FRAME_POS, D))
    q_four = q_norm.reshape(FRAMES, FRAME_POS, HEADS, HEAD_DIM)
    k_four = k_norm.reshape(FRAMES, FRAME_POS, HEADS, HEAD_DIM)
    v_four = values.reshape(FRAMES, FRAME_POS, HEADS, HEAD_DIM)
    query_span = math.gcd(FRAME_POS, 512)

    def spatial_frame(triple):
        q_blocks = triple[0].reshape(FRAME_POS // query_span, query_span, HEADS, HEAD_DIM)
        result = lax.map(lambda q_part: attend(q_part, triple[1], triple[2]), q_blocks)
        return result.reshape(FRAME_POS, HEADS, HEAD_DIM)
    spatial = lax.map(spatial_frame, (q_four, k_four, v_four))
    span = math.gcd(FRAME_POS, 64)

    def by_position(array_in):
        return array_in.transpose(1, 0, 2, 3).reshape(FRAME_POS // span, span, FRAMES, HEADS, HEAD_DIM)
    temporal = lax.map(lambda triple: attend(triple[0], triple[1], triple[2]), (by_position(q_four), by_position(k_four), by_position(v_four)))
    temporal = temporal.reshape(FRAME_POS, FRAMES, HEADS, HEAD_DIM).astype(jnp.bfloat16)
    temporal = lax.optimization_barrier(temporal).astype(jnp.float32).transpose(1, 0, 2, 3)
    return (spatial + temporal).reshape(TOKENS, D).astype(jnp.bfloat16)
```

```python
import math

import jax
import jax.numpy as jnp
from jax import lax
from jax.experimental import pallas as pl
from jax.experimental.pallas import tpu as pltpu
from jax.sharding import Mesh, PartitionSpec as P

D = 5120
HEAD = 128
EPS = 1e-06
SCALE = 1.0 / math.sqrt(HEAD)
SEQ = ("x", "yl", "zh", "zl", "c")
FRAME = ("x", "yl", "zh")


def contract_last(a, b):
    return lax.dot_general(a, b, (((1,), (1,)), ((), ())), preferred_element_type=jnp.float32)


def softmax_times(scores, v):
    top = jnp.max(scores, axis=-1, keepdims=True)
    raised = jnp.exp((scores - top) * SCALE)
    total = jnp.sum(raised, axis=-1, keepdims=True)
    out = jnp.dot(raised.astype(jnp.bfloat16), v, preferred_element_type=jnp.float32)
    return out / total


def normed(x, stat, gain):
    scale = lax.rsqrt(stat / D + EPS)
    return (x.astype(jnp.float32) * scale * gain).astype(jnp.bfloat16)


def spatial_kernel(q_ref, qs_ref, ks_ref, qg_ref, kg_ref, b0, b1, b2, b3, out_ref, k_all, v_all):
    n = q_ref.shape[0]
    for i, blk in enumerate((b0, b1, b2, b3)):
        rows = pl.ds(i * n, n)
        k_all[rows, :] = normed(blk[pl.ds(0, n), :], ks_ref[rows, :], kg_ref[...])
        v_all[rows, :] = blk[pl.ds(n, n), :]
    q = normed(q_ref[...], qs_ref[...], qg_ref[...])
    out_ref[...] = softmax_times(contract_last(q, k_all[...]), v_all[...])


def spatial(q, qs, ks, qg, kg, blocks):
    n, width = q.shape
    heads = width // HEAD
    col = lambda rows: pl.BlockSpec((rows, HEAD), lambda h: (0, h))
    whole = lambda rows: pl.BlockSpec((rows, 1), lambda h: (0, 0))
    return pl.pallas_call(
        spatial_kernel,
        grid=(heads,),
        out_shape=jax.ShapeDtypeStruct((n, width), jnp.float32),
        in_specs=[col(n), whole(n), whole(4 * n), col(1), col(1)] + [col(2 * n)] * 4,
        out_specs=col(n),
        scratch_shapes=[
            pltpu.VMEM((4 * n, HEAD), jnp.bfloat16),
            pltpu.VMEM((4 * n, HEAD), jnp.bfloat16),
        ],
        compiler_params=pltpu.CompilerParams(vmem_limit_bytes=24 << 20),
        cost_estimate=pl.CostEstimate(
            flops=heads * n * n * 4 * HEAD * 4, bytes_accessed=n * width * 22, transcendentals=heads * n * n * 4
        ),
    )(q, qs, ks, qg, kg, *blocks)


def temporal_kernel(q_ref, k_ref, v_ref, out_ref, *, per):
    n = q_ref.shape[0]
    row = lax.broadcasted_iota(jnp.int32, (n, n), 0)
    column = lax.broadcasted_iota(jnp.int32, (n, n), 1)
    same = (row - column) % per == 0
    scores = contract_last(q_ref[...], k_ref[...])
    scores = jnp.where(same, scores, -1e30)
    out_ref[...] = softmax_times(scores, v_ref[...]).astype(jnp.bfloat16)


def temporal(q, k, v, per):
    n, width = q.shape
    heads = width // HEAD
    col = pl.BlockSpec((n, HEAD), lambda h: (0, h))
    return pl.pallas_call(
        lambda *refs: temporal_kernel(*refs, per=per),
        grid=(heads,),
        out_shape=jax.ShapeDtypeStruct((n, width), jnp.bfloat16),
        in_specs=[col] * 3,
        out_specs=col,
        compiler_params=pltpu.CompilerParams(vmem_limit_bytes=24 << 20),
        cost_estimate=pl.CostEstimate(
            flops=heads * n * n * HEAD * 4, bytes_accessed=n * width * 8, transcendentals=heads * n * n
        ),
    )(q, k, v)


def per_device(queries, keys, values, query_gain, key_gain):
    tok, width = queries.shape
    half = width // 2
    zl, core = lax.axis_index("zl"), lax.axis_index("c")
    frames = lax.axis_size(FRAME)

    def mine(a):
        return lax.dynamic_slice_in_dim(a, core * half, half, a.ndim - 1)

    def other(a):
        return lax.dynamic_slice_in_dim(a, (1 - core) * half, half, a.ndim - 1)

    swap = [(0, 1), (1, 0)]
    sent = jnp.concatenate([other(keys), other(values), other(queries)], axis=0)
    got = lax.ppermute(sent, "c", swap)
    own_kv = jnp.concatenate([mine(keys), got[:tok], mine(values), got[tok : 2 * tok]], axis=0)
    own_q = jnp.concatenate([mine(queries), got[2 * tok :]], axis=0)

    up = [(i, i + 1) for i in range(3)]
    down = [(i + 1, i) for i in range(3)]
    plus1 = lax.ppermute(own_kv, "zl", up)
    minus1 = lax.ppermute(own_kv, "zl", down)
    plus2 = lax.ppermute(plus1, "zl", up[1:])
    minus2 = lax.ppermute(minus1, "zl", down[:-1])
    plus3 = lax.ppermute(plus2, "zl", up[2:])
    minus3 = lax.ppermute(minus2, "zl", down[:1])

    part = jnp.stack(
        [
            jnp.sum(jnp.square(queries.astype(jnp.float32)), axis=1),
            jnp.sum(jnp.square(keys.astype(jnp.float32)), axis=1),
        ]
    )
    place = lax.broadcasted_iota(jnp.int32, (8, 1, 1), 0) == zl * 2 + core
    stats = lax.psum(jnp.where(place, part[None], 0.0), ("tp", "zl", "c"))
    stat_of = lambda z, c: lax.dynamic_index_in_dim(stats, z * 2 + c, 0, keepdims=False)
    own_stat, twin_stat = stat_of(zl, core), stat_of(zl, 1 - core)
    q_norm = normed(queries, own_stat[0][:, None], query_gain[None, :])
    k_norm = normed(keys, own_stat[1][:, None], key_gain[None, :])

    def to_positions(a):
        return lax.all_to_all(a.reshape(frames, tok // frames, width), FRAME, 0, 0, tiled=True)

    tq, tk, tv = (to_positions(a).reshape(tok, width) for a in (q_norm, k_norm, values))
    t_out = temporal(tq, tk, tv, tok // frames)
    t_back = to_positions(t_out).reshape(tok, width)

    blocks = [
        own_kv,
        jnp.where(zl >= 1, plus1, minus3),
        jnp.where(zl >= 2, plus2, minus2),
        jnp.where(zl >= 3, plus3, minus1),
    ]
    q_stat = jnp.concatenate([own_stat[0], twin_stat[0]])[:, None]
    k_stat = jnp.concatenate(
        [stat_of((zl - j) % 4, c)[1] for j in range(4) for c in (core, 1 - core)]
    )[:, None]
    s_out = spatial(own_q, q_stat, k_stat, mine(query_gain)[None], mine(key_gain)[None], blocks)
    s_got = lax.ppermute(s_out[tok:], "c", swap)
    s_mine = s_out[:tok]
    s_all = jnp.where(
        core == 0,
        jnp.concatenate([s_mine, s_got], axis=1),
        jnp.concatenate([s_got, s_mine], axis=1),
    )
    return (s_all + t_back.astype(jnp.float32)).astype(jnp.bfloat16)


def solution(mesh):
    axes = SEQ + ("tp",)
    split = Mesh(mesh.devices.reshape(4, 2, 2, 4, 2, 4), axes)
    return jax.shard_map(
        per_device,
        mesh=split,
        in_specs=(P(SEQ, "tp"), P(SEQ, "tp"), P(SEQ, "tp"), P("tp"), P("tp")),
        out_specs=P(SEQ, "tp"),
        check_vma=False,
    )
```

```python
import math

import jax
import jax.numpy as jnp
from jax import lax
from jax.experimental import pallas as pl
from jax.experimental.pallas import tpu as pltpu
from jax.sharding import Mesh, PartitionSpec as P

D = 5120
HEAD = 128
EPS = 1e-06
SCALE = 1.0 / math.sqrt(HEAD)
SEQ = ("x", "yl", "zh", "zl", "c")
FRAME = ("x", "yl", "zh")


def contract_last(a, b):
    return lax.dot_general(a, b, (((1,), (1,)), ((), ())), preferred_element_type=jnp.float32)


def softmax_times(scores, v):
    top = jnp.max(scores, axis=-1, keepdims=True)
    raised = jnp.exp((scores - top) * SCALE)
    total = jnp.sum(raised, axis=-1, keepdims=True)
    out = jnp.dot(raised.astype(jnp.bfloat16), v, preferred_element_type=jnp.float32)
    return out / total


def normed(x, stat, gain):
    scale = lax.rsqrt(stat / D + EPS)
    return (x.astype(jnp.float32) * scale * gain).astype(jnp.bfloat16)


def spatial_kernel(zl_ref, q_ref, qs_ref, ks_ref, qg_ref, kg_ref, own, p1, m3, p2, m2, p3, m1, out_ref, k_all, v_all):
    n, width = q_ref.shape
    zl = zl_ref[0]
    pairs = ((own, None), (p1, m3), (p2, m2), (p3, m1))
    for h in range(width // HEAD):
        col = pl.ds(h * HEAD, HEAD)
        for i, (low, high) in enumerate(pairs):
            rows = pl.ds(i * n, n)

            def fill(blk, rows=rows, col=col):
                k_all[rows, :] = normed(blk[pl.ds(0, n), col], ks_ref[rows, :], kg_ref[:, col])
                v_all[rows, :] = blk[pl.ds(n, n), col]

            if high is None:
                fill(low)
            else:
                pl.when(zl >= i)(lambda low=low: fill(low))
                pl.when(zl < i)(lambda high=high: fill(high))
        q = normed(q_ref[:, col], qs_ref[...], qg_ref[:, col])
        out_ref[:, col] = softmax_times(contract_last(q, k_all[...]), v_all[...])


def spatial(zl, q, qs, ks, qg, kg, blocks):
    n, width = q.shape
    heads = width // HEAD
    vmem = pl.BlockSpec(memory_space=pltpu.VMEM)
    return pl.pallas_call(
        spatial_kernel,
        out_shape=jax.ShapeDtypeStruct((n, width), jnp.float32),
        in_specs=[pl.BlockSpec(memory_space=pltpu.SMEM)] + [vmem] * (5 + len(blocks)),
        out_specs=vmem,
        scratch_shapes=[
            pltpu.VMEM((4 * n, HEAD), jnp.bfloat16),
            pltpu.VMEM((4 * n, HEAD), jnp.bfloat16),
        ],
        compiler_params=pltpu.CompilerParams(vmem_limit_bytes=40 << 20),
        cost_estimate=pl.CostEstimate(
            flops=heads * n * n * 4 * HEAD * 4, bytes_accessed=n * width * 22, transcendentals=heads * n * n * 4
        ),
    )(zl, q, qs, ks, qg, kg, *blocks)


def temporal_kernel(x_ref, out_ref, *, per):
    n, width = out_ref.shape
    row = lax.broadcasted_iota(jnp.int32, (n, n), 0)
    column = lax.broadcasted_iota(jnp.int32, (n, n), 1)
    same = (row - column) % per == 0
    for h in range(width // HEAD):
        q, k, v = (x_ref[:, pl.ds(i * width + h * HEAD, HEAD)] for i in range(3))
        scores = jnp.where(same, contract_last(q, k), -1e30)
        out_ref[:, pl.ds(h * HEAD, HEAD)] = softmax_times(scores, v).astype(jnp.bfloat16)


def temporal(x, per):
    n, width = x.shape
    width = width // 3
    heads = width // HEAD
    vmem = pl.BlockSpec(memory_space=pltpu.VMEM)
    return pl.pallas_call(
        lambda *refs: temporal_kernel(*refs, per=per),
        out_shape=jax.ShapeDtypeStruct((n, width), jnp.bfloat16),
        in_specs=[vmem],
        out_specs=vmem,
        compiler_params=pltpu.CompilerParams(vmem_limit_bytes=24 << 20),
        cost_estimate=pl.CostEstimate(
            flops=heads * n * n * HEAD * 4, bytes_accessed=n * width * 8, transcendentals=heads * n * n
        ),
    )(x)


def per_device(queries, keys, values, query_gain, key_gain):
    tok, width = queries.shape
    half = width // 2
    zl, core = lax.axis_index("zl"), lax.axis_index("c")
    frames = lax.axis_size(FRAME)

    def mine(a):
        return lax.dynamic_slice_in_dim(a, core * half, half, a.ndim - 1)

    def other(a):
        return lax.dynamic_slice_in_dim(a, (1 - core) * half, half, a.ndim - 1)

    swap = [(0, 1), (1, 0)]
    sent = jnp.concatenate([other(keys), other(values), other(queries)], axis=0)
    got = lax.ppermute(sent, "c", swap)
    part = jnp.stack(
        [
            jnp.sum(jnp.square(queries.astype(jnp.float32)), axis=1),
            jnp.sum(jnp.square(keys.astype(jnp.float32)), axis=1),
        ]
    )
    own_kv = jnp.concatenate([mine(keys), got[:tok], mine(values), got[tok : 2 * tok]], axis=0)
    own_q = jnp.concatenate([mine(queries), got[2 * tok :]], axis=0)
    part, own_kv = lax.optimization_barrier((part, own_kv))

    up = [(i, i + 1) for i in range(3)]
    down = [(i + 1, i) for i in range(3)]
    plus1 = lax.ppermute(own_kv, "zl", up)
    minus1 = lax.ppermute(own_kv, "zl", down)
    plus2 = lax.ppermute(plus1, "zl", up[1:])
    minus2 = lax.ppermute(minus1, "zl", down[:-1])
    plus3 = lax.ppermute(plus2, "zl", up[2:])
    minus3 = lax.ppermute(minus2, "zl", down[:1])

    stat = lax.psum(part, "tp")
    q_norm = normed(queries, stat[0][:, None], query_gain[None, :])
    k_norm = normed(keys, stat[1][:, None], key_gain[None, :])
    twin = lax.ppermute(stat, "c", swap)
    both = jnp.concatenate([stat[1], twin[1]])
    k_stats = [both] + [
        lax.ppermute(both, "zl", [(i, (i + j) % 4) for i in range(4)]) for j in range(1, 4)
    ]

    def to_positions(a):
        sent = a.reshape(frames, tok // frames, a.shape[1])
        return lax.all_to_all(sent, FRAME, 0, 0, tiled=True).reshape(a.shape)

    t_in = to_positions(jnp.concatenate([q_norm, k_norm, values], axis=1))
    t_back = to_positions(temporal(t_in, tok // frames))

    blocks = [own_kv, plus1, minus3, plus2, minus2, plus3, minus1]
    q_stat = jnp.concatenate([stat[0], twin[0]])[:, None]
    k_stat = jnp.concatenate(k_stats)[:, None]
    s_out = spatial(
        zl.reshape(1), own_q, q_stat, k_stat, mine(query_gain)[None], mine(key_gain)[None], blocks
    )
    s_got = lax.ppermute(s_out[tok:], "c", swap)
    s_mine = s_out[:tok]
    s_all = jnp.where(
        core == 0,
        jnp.concatenate([s_mine, s_got], axis=1),
        jnp.concatenate([s_got, s_mine], axis=1),
    )
    return (s_all + t_back.astype(jnp.float32)).astype(jnp.bfloat16)


def solution(mesh):
    axes = SEQ + ("tp",)
    split = Mesh(mesh.devices.reshape(4, 2, 2, 4, 2, 4), axes)
    return jax.shard_map(
        per_device,
        mesh=split,
        in_specs=(P(SEQ, "tp"), P(SEQ, "tp"), P(SEQ, "tp"), P("tp"), P("tp")),
        out_specs=P(SEQ, "tp"),
        check_vma=False,
    )
```

```python
import math

import jax
import jax.numpy as jnp
from jax import lax
from jax.experimental import pallas as pl
from jax.experimental.pallas import tpu as pltpu
from jax.sharding import Mesh, PartitionSpec as P

D = 5120
HEAD = 128
EPS = 1e-06
SCALE = 1.0 / math.sqrt(HEAD)
SEQ = ("x", "yl", "zh", "zl", "c")
FRAME = ("x", "yl", "zh")


def contract_last(a, b):
    return lax.dot_general(a, b, (((1,), (1,)), ((), ())), preferred_element_type=jnp.float32)


def softmax_times(scores, v):
    top = jnp.max(scores, axis=-1, keepdims=True)
    raised = jnp.exp((scores - top) * SCALE)
    total = jnp.sum(raised, axis=-1, keepdims=True)
    out = jnp.dot(raised.astype(jnp.bfloat16), v, preferred_element_type=jnp.float32)
    return out / total


def normed(x, stat, gain):
    scale = lax.rsqrt(stat / D + EPS)
    return (x.astype(jnp.float32) * scale * gain).astype(jnp.bfloat16)


def prep_kernel(at_ref, q_ref, k_ref, v_ref, p0, p1, p2, p3, sum_ref):
    n, width = q_ref.shape
    half = width // 2
    for j, out in enumerate((p0, p1, p2, p3)):
        h = lax.rem(at_ref[0] + j, 4) * HEAD
        for c, side in enumerate((at_ref[1], 1 - at_ref[1])):
            moving = pl.ds(pl.multiple_of(side * half + h, HEAD), HEAD)
            staying = pl.ds(pl.multiple_of((side + 1) * half - HEAD, HEAD), HEAD)
            parts = ((q_ref, moving), (k_ref, moving), (v_ref, moving), (k_ref, staying), (v_ref, staying))
            for i, (ref, col) in enumerate(parts):
                out[:, c * half + i * HEAD : c * half + (i + 1) * HEAD] = ref[:, col]
    ones = jnp.ones((4, HEAD), jnp.float32)
    for i, ref in enumerate((q_ref, k_ref)):
        total = jnp.zeros((n, HEAD), jnp.float32)
        for h in range(width // HEAD):
            total += jnp.square(ref[:, h * HEAD : (h + 1) * HEAD].astype(jnp.float32))
        sum_ref[i * 4 : (i + 1) * 4, :] = lax.dot_general(
            ones,
            total,
            (((1,), (1,)), ((), ())),
            precision=lax.Precision.HIGHEST,
            preferred_element_type=jnp.float32,
        )


def prep(at, q, k, v):
    vmem = pl.BlockSpec(memory_space=pltpu.VMEM)
    return pl.pallas_call(
        prep_kernel,
        out_shape=[jax.ShapeDtypeStruct(q.shape, q.dtype)] * 4
        + [jax.ShapeDtypeStruct((8, q.shape[0]), jnp.float32)],
        in_specs=[pl.BlockSpec(memory_space=pltpu.SMEM)] + [vmem] * 3,
        out_specs=[vmem] * 5,
        compiler_params=pltpu.CompilerParams(vmem_limit_bytes=24 << 20),
        cost_estimate=pl.CostEstimate(flops=q.size * 4, bytes_accessed=q.size * 14, transcendentals=0),
    )(at, q, k, v)


def spatial_kernel(at_ref, b0, b1, b2, b3, q_last, s0, s2, s3, stat_ref, qg_ref, kg_ref, o0, o1, o2, o3, o_last, q_all, k_all, v_all):
    n, half = b0.shape[0], b0.shape[1] // 2
    zl, core = at_ref[0], at_ref[1]
    moving = pl.ds(pl.multiple_of(core * half + zl * HEAD, HEAD), HEAD)
    staying = pl.ds(pl.multiple_of(core * half + half - HEAD, HEAD), HEAD)
    q_gain, q_gain_last = qg_ref[:, moving], qg_ref[:, staying]
    k_gain, k_gain_last = kg_ref[:, moving], kg_ref[:, staying]
    for j, blk in enumerate((b0, b1, b2, b3)):
        for twin in range(2):

            def part(i):
                if twin:
                    ref, at = ((s0, 0), (s0, half), (s2, 0), (s3, 0))[j]
                    return ref[:, at + i * HEAD : at + (i + 1) * HEAD]
                return blk[:, i * HEAD : (i + 1) * HEAD]

            rows = slice((j * 2 + twin) * n, (j * 2 + twin + 1) * n)
            place = lax.rem(zl + 4 - j, 4) * 2 + (1 - core if twin else core)
            from_rows = pl.ds(pl.multiple_of(place * n, n), n)
            q_stat, k_stat = stat_ref[from_rows, 0:1], stat_ref[from_rows, 1:2]
            q_all[rows, 0:HEAD] = normed(part(0), q_stat, q_gain)
            k_all[rows, 0:HEAD] = normed(part(1), k_stat, k_gain)
            v_all[rows, 0:HEAD] = part(2)
            k_all[rows, HEAD:] = normed(part(3), k_stat, k_gain_last)
            v_all[rows, HEAD:] = part(4)
            if j == 0:
                q = s0[:, 2 * half :] if twin else q_last[...]
                q_all[rows, HEAD:] = normed(q, q_stat, q_gain_last)
    k_one, k_two = k_all[:, 0:HEAD], k_all[:, HEAD:]
    v_one, v_two = v_all[:, 0:HEAD], v_all[:, HEAD:]
    for j, out in enumerate((o0, o1, o2, o3)):
        q = q_all[j * 2 * n : (j + 1) * 2 * n, 0:HEAD]
        out[...] = softmax_times(contract_last(q, k_one), v_one).astype(jnp.bfloat16)
    o_last[...] = softmax_times(contract_last(q_all[0 : 2 * n, HEAD:], k_two), v_two).astype(jnp.bfloat16)


def spatial(at, blocks, q_last, swapped, stats, q_gain, k_gain):
    n = blocks[0].shape[0]
    vmem = pl.BlockSpec(memory_space=pltpu.VMEM)
    return pl.pallas_call(
        spatial_kernel,
        out_shape=[jax.ShapeDtypeStruct((2 * n, HEAD), jnp.bfloat16)] * 5,
        in_specs=[pl.BlockSpec(memory_space=pltpu.SMEM)] + [vmem] * 11,
        out_specs=[vmem] * 5,
        scratch_shapes=[pltpu.VMEM((8 * n, 2 * HEAD), jnp.bfloat16)] * 3,
        compiler_params=pltpu.CompilerParams(vmem_limit_bytes=40 << 20),
        cost_estimate=pl.CostEstimate(
            flops=5 * n * n * 64 * HEAD, bytes_accessed=n * HEAD * 120, transcendentals=5 * n * n * 16
        ),
    )(at, *blocks, q_last, *swapped, stats, q_gain, k_gain)


def temporal_kernel(x_ref, out_ref, *, per):
    n, width = out_ref.shape
    row = lax.broadcasted_iota(jnp.int32, (n, n), 0)
    column = lax.broadcasted_iota(jnp.int32, (n, n), 1)
    same = (row - column) % per == 0
    for h in range(width // HEAD):
        q, k, v = (x_ref[:, pl.ds(i * width + h * HEAD, HEAD)] for i in range(3))
        scores = jnp.where(same, contract_last(q, k), -1e30)
        out_ref[:, pl.ds(h * HEAD, HEAD)] = softmax_times(scores, v).astype(jnp.bfloat16)


def temporal(x, per):
    n, width = x.shape
    width = width // 3
    heads = width // HEAD
    vmem = pl.BlockSpec(memory_space=pltpu.VMEM)
    return pl.pallas_call(
        lambda *refs: temporal_kernel(*refs, per=per),
        out_shape=jax.ShapeDtypeStruct((n, width), jnp.bfloat16),
        in_specs=[vmem],
        out_specs=vmem,
        compiler_params=pltpu.CompilerParams(vmem_limit_bytes=24 << 20),
        cost_estimate=pl.CostEstimate(
            flops=heads * n * n * HEAD * 4, bytes_accessed=n * width * 8, transcendentals=heads * n * n
        ),
    )(x)


def per_device(queries, keys, values, query_gain, key_gain):
    tok, width = queries.shape
    half = width // 2
    zl, core = lax.axis_index("zl"), lax.axis_index("c")
    frames = lax.axis_size(FRAME)
    swap = [(0, 1), (1, 0)]

    def shift(a, j):
        return lax.ppermute(a, "zl", [(i, (i + j) % 4) for i in range(4)])

    def column(a, start, size=HEAD):
        return lax.dynamic_slice_in_dim(a, start, size, 1)

    def to_positions(a):
        sent = a.reshape(frames, tok // frames, a.shape[1])
        return lax.all_to_all(sent, FRAME, 0, 0, tiled=True).reshape(a.shape)

    at = jnp.stack([zl, core])
    *parts, sums = prep(at, queries, keys, values)
    blocks = [parts[0]] + [shift(parts[j], j) for j in (1, 2, 3)]
    sums = lax.psum(sums, "tp")

    q_norm = normed(queries, sums[0][:, None], query_gain[None, :])
    k_norm = normed(keys, sums[4][:, None], key_gain[None, :])
    t_sent = jnp.concatenate([q_norm, k_norm, values], axis=1)
    stat = jnp.stack([sums[0], sums[4]])
    stats = lax.all_gather(stat, ("zl", "c")).transpose(0, 2, 1).reshape(8 * tok, 2)
    t_sent, blocks, stats = lax.optimization_barrier((t_sent, blocks, stats))
    t_in = to_positions(t_sent)

    away = [b[:, half:] for b in blocks]
    q_away = column(queries, (2 - core) * half - HEAD)
    swapped = [
        lax.ppermute(a, "c", swap)
        for a in (jnp.concatenate([away[0], away[1], q_away], axis=1), away[2], away[3])
    ]
    outs = spatial(
        at,
        blocks,
        column(queries, (core + 1) * half - HEAD),
        swapped,
        stats,
        query_gain[None],
        key_gain[None],
    )
    t_in, last = lax.optimization_barrier((t_in, outs[4]))
    t_out = temporal(t_in, tok // frames)
    t_back = to_positions(t_out)

    moved = [shift(outs[j], 4 - j) for j in (1, 2, 3)]
    moved, t_out = lax.optimization_barrier((moved, t_out))
    heads = [outs[0]] + moved
    turned = column(jnp.concatenate(heads + heads[:3], axis=1), (4 - zl) % 4 * HEAD, 4 * HEAD)
    s_half = jnp.concatenate([turned, last], axis=1)
    s_got = lax.ppermute(s_half[tok:], "c", swap)
    s_mine = s_half[:tok]
    s_all = jnp.where(
        core == 0,
        jnp.concatenate([s_mine, s_got], axis=1),
        jnp.concatenate([s_got, s_mine], axis=1),
    )
    return (s_all.astype(jnp.float32) + t_back.astype(jnp.float32)).astype(jnp.bfloat16)


def solution(mesh):
    axes = SEQ + ("tp",)
    split = Mesh(mesh.devices.reshape(4, 2, 2, 4, 2, 4), axes)
    return jax.shard_map(
        per_device,
        mesh=split,
        in_specs=(P(SEQ, "tp"), P(SEQ, "tp"), P(SEQ, "tp"), P("tp"), P("tp")),
        out_specs=P(SEQ, "tp"),
        check_vma=False,
    )
```

```python
import math

import jax
import jax.numpy as jnp
from jax import lax
from jax.experimental import pallas as pl
from jax.experimental.pallas import tpu as pltpu
from jax.sharding import Mesh, PartitionSpec as P

D = 5120
HEAD = 128
EPS = 1e-06
SCALE = 1.0 / math.sqrt(HEAD)
SEQ = ("x", "yl", "zh", "zl", "c")
FRAME = ("x", "yl", "zh")


def contract_last(a, b):
    return lax.dot_general(a, b, (((1,), (1,)), ((), ())), preferred_element_type=jnp.float32)


def softmax_times(scores, v):
    top = jnp.max(scores, axis=-1, keepdims=True)
    raised = jnp.exp((scores - top) * SCALE)
    total = jnp.sum(raised, axis=-1, keepdims=True)
    out = jnp.dot(raised.astype(jnp.bfloat16), v, preferred_element_type=jnp.float32)
    return out / total


def normed(x, stat, gain):
    scale = lax.rsqrt(stat / D + EPS)
    return (x.astype(jnp.float32) * scale * gain).astype(jnp.bfloat16)


def prep_kernel(at_ref, q_hbm, k_hbm, v_hbm, p0, p1, p2, p3, keep_ref, sum_ref, x_ref, sems):
    n, width = q_hbm.shape
    loads = []
    for i, src in enumerate((q_hbm, k_hbm, v_hbm)):
        for r in range(2):
            rows = pl.ds(r * (n // 2), n // 2)
            dst = x_ref.at[rows, pl.ds(i * width, width)]
            loads.append(pltpu.make_async_copy(src.at[rows], dst, sems.at[i * 2 + r]))
    for load in loads:
        load.start()
    for load in loads:
        load.wait()
    half = width // 2
    for j, out in enumerate((p0, p1, p2, p3)):
        h = lax.rem(at_ref[0] + j, 4) * HEAD
        for c, side in enumerate((at_ref[1], 1 - at_ref[1])):
            moving, staying = side * half + h, (side + 1) * half - HEAD
            five = ((0, moving), (1, moving), (2, moving), (1, staying), (2, staying))
            for i, (a, start) in enumerate(five):
                col = pl.ds(pl.multiple_of(a * width + start, HEAD), HEAD)
                out[:, c * half + i * HEAD : c * half + (i + 1) * HEAD] = x_ref[:, col]
    for c, side in enumerate((at_ref[1], 1 - at_ref[1])):
        staying = pl.ds(pl.multiple_of((side + 1) * half - HEAD, HEAD), HEAD)
        keep_ref[:, c * HEAD : (c + 1) * HEAD] = x_ref[:, staying]
    ones = jnp.ones((4, HEAD), jnp.float32)
    for i in range(2):
        total = jnp.zeros((n, HEAD), jnp.float32)
        for h in range(width // HEAD):
            start = i * width + h * HEAD
            total += jnp.square(x_ref[:, start : start + HEAD].astype(jnp.float32))
        sum_ref[i * 4 : (i + 1) * 4, :] = lax.dot_general(
            ones,
            total,
            (((1,), (1,)), ((), ())),
            precision=lax.Precision.HIGHEST,
            preferred_element_type=jnp.float32,
        )


def prep(at, q, k, v):
    vmem = pl.BlockSpec(memory_space=pltpu.VMEM)
    return pl.pallas_call(
        prep_kernel,
        out_shape=[jax.ShapeDtypeStruct(q.shape, q.dtype)] * 4
        + [
            jax.ShapeDtypeStruct((q.shape[0], 2 * HEAD), q.dtype),
            jax.ShapeDtypeStruct((8, q.shape[0]), jnp.float32),
            jax.ShapeDtypeStruct((q.shape[0], 3 * q.shape[1]), q.dtype),
        ],
        in_specs=[pl.BlockSpec(memory_space=pltpu.SMEM)] + [pl.BlockSpec(memory_space=pltpu.HBM)] * 3,
        out_specs=[vmem] * 7,
        scratch_shapes=[pltpu.SemaphoreType.DMA((6,))],
        compiler_params=pltpu.CompilerParams(vmem_limit_bytes=24 << 20),
        cost_estimate=pl.CostEstimate(flops=q.size * 4, bytes_accessed=q.size * 14, transcendentals=0),
    )(at, q, k, v)


def norm_kernel(x_ref, sum_ref, qg_ref, kg_ref, t_ref):
    n, width = x_ref.shape[0], x_ref.shape[1] // 3
    for i, gain in enumerate((qg_ref, kg_ref)):
        stat = jnp.broadcast_to(sum_ref[i * 4 : i * 4 + 1, :], (n, n)).T
        scale = lax.rsqrt(stat / D + EPS)
        for h in range(width // HEAD):
            here = slice(i * width + h * HEAD, i * width + (h + 1) * HEAD)
            value = x_ref[:, here].astype(jnp.float32) * scale * gain[:, h * HEAD : (h + 1) * HEAD]
            t_ref[:, here] = value.astype(jnp.bfloat16)
    t_ref[:, 2 * width :] = x_ref[:, 2 * width :]


def norm(x, sums, q_gain, k_gain):
    vmem = pl.BlockSpec(memory_space=pltpu.VMEM)
    return pl.pallas_call(
        norm_kernel,
        out_shape=jax.ShapeDtypeStruct(x.shape, x.dtype),
        in_specs=[vmem] * 4,
        out_specs=vmem,
        compiler_params=pltpu.CompilerParams(vmem_limit_bytes=24 << 20),
        cost_estimate=pl.CostEstimate(flops=x.size * 3, bytes_accessed=x.size * 4, transcendentals=0),
    )(x, sums, q_gain, k_gain)


def pack_kernel(b0, b1, b2, b3, keep, out):
    half = b0.shape[1] // 2
    for j, blk in enumerate((b0, b1, b2, b3)):
        out[:, j * half : (j + 1) * half] = blk[:, half:]
    out[:, 4 * half :] = keep[:, HEAD:]


def pack(blocks, keep):
    n, width = blocks[0].shape
    vmem = pl.BlockSpec(memory_space=pltpu.VMEM)
    return pl.pallas_call(
        pack_kernel,
        out_shape=jax.ShapeDtypeStruct((n, 2 * width + HEAD), keep.dtype),
        in_specs=[vmem] * 5,
        out_specs=vmem,
        compiler_params=pltpu.CompilerParams(vmem_limit_bytes=24 << 20),
        cost_estimate=pl.CostEstimate(flops=0, bytes_accessed=n * width * 8, transcendentals=0),
    )(*blocks, keep)


def spatial_kernel(at_ref, b0, b1, b2, b3, keep, sw_ref, stat_ref, qg_ref, kg_ref, o0, o1, o2, o3, o_last, q_all, k_all, v_all):
    n, half = b0.shape[0], b0.shape[1] // 2
    zl, core = at_ref[0], at_ref[1]
    moving = pl.ds(pl.multiple_of(core * half + zl * HEAD, HEAD), HEAD)
    staying = pl.ds(pl.multiple_of(core * half + half - HEAD, HEAD), HEAD)
    q_gain, q_gain_last = qg_ref[:, moving], qg_ref[:, staying]
    k_gain, k_gain_last = kg_ref[:, moving], kg_ref[:, staying]
    for j, blk in enumerate((b0, b1, b2, b3)):
        for twin in range(2):

            def part(i):
                if twin:
                    return sw_ref[:, j * half + i * HEAD : j * half + (i + 1) * HEAD]
                return blk[:, i * HEAD : (i + 1) * HEAD]

            rows = slice((j * 2 + twin) * n, (j * 2 + twin + 1) * n)
            place = lax.rem(zl + 4 - j, 4) * 2 + (1 - core if twin else core)
            from_rows = pl.ds(pl.multiple_of(place * n, n), n)
            q_stat, k_stat = stat_ref[from_rows, 0:1], stat_ref[from_rows, 1:2]
            q_all[rows, 0:HEAD] = normed(part(0), q_stat, q_gain)
            k_all[rows, 0:HEAD] = normed(part(1), k_stat, k_gain)
            v_all[rows, 0:HEAD] = part(2)
            k_all[rows, HEAD:] = normed(part(3), k_stat, k_gain_last)
            v_all[rows, HEAD:] = part(4)
            if j == 0:
                q = sw_ref[:, 4 * half :] if twin else keep[:, 0:HEAD]
                q_all[rows, HEAD:] = normed(q, q_stat, q_gain_last)
    k_one, k_two = k_all[:, 0:HEAD], k_all[:, HEAD:]
    v_one, v_two = v_all[:, 0:HEAD], v_all[:, HEAD:]
    for j, out in enumerate((o0, o1, o2, o3)):
        q = q_all[j * 2 * n : (j + 1) * 2 * n, 0:HEAD]
        out[...] = softmax_times(contract_last(q, k_one), v_one).astype(jnp.bfloat16)
    o_last[...] = softmax_times(contract_last(q_all[0 : 2 * n, HEAD:], k_two), v_two).astype(jnp.bfloat16)


def spatial(at, blocks, keep, swapped, stats, q_gain, k_gain):
    n = blocks[0].shape[0]
    vmem = pl.BlockSpec(memory_space=pltpu.VMEM)
    return pl.pallas_call(
        spatial_kernel,
        out_shape=[jax.ShapeDtypeStruct((2 * n, HEAD), jnp.bfloat16)] * 5,
        in_specs=[pl.BlockSpec(memory_space=pltpu.SMEM)] + [vmem] * 9,
        out_specs=[vmem] * 5,
        scratch_shapes=[pltpu.VMEM((8 * n, 2 * HEAD), jnp.bfloat16)] * 3,
        compiler_params=pltpu.CompilerParams(vmem_limit_bytes=40 << 20),
        cost_estimate=pl.CostEstimate(
            flops=5 * n * n * 64 * HEAD, bytes_accessed=n * HEAD * 120, transcendentals=5 * n * n * 16
        ),
    )(at, *blocks, keep, swapped, stats, q_gain, k_gain)


def temporal_kernel(x_ref, out_ref, *, per):
    n, width = out_ref.shape
    row = lax.broadcasted_iota(jnp.int32, (n, n), 0)
    column = lax.broadcasted_iota(jnp.int32, (n, n), 1)
    same = (row - column) % per == 0
    for h in range(width // HEAD):
        q, k, v = (x_ref[:, pl.ds(i * width + h * HEAD, HEAD)] for i in range(3))
        scores = jnp.where(same, contract_last(q, k), -1e30)
        out_ref[:, pl.ds(h * HEAD, HEAD)] = softmax_times(scores, v).astype(jnp.bfloat16)


def temporal(x, per):
    n, width = x.shape
    width = width // 3
    heads = width // HEAD
    vmem = pl.BlockSpec(memory_space=pltpu.VMEM)
    return pl.pallas_call(
        lambda *refs: temporal_kernel(*refs, per=per),
        out_shape=jax.ShapeDtypeStruct((n, width), jnp.bfloat16),
        in_specs=[vmem],
        out_specs=vmem,
        compiler_params=pltpu.CompilerParams(vmem_limit_bytes=24 << 20),
        cost_estimate=pl.CostEstimate(
            flops=heads * n * n * HEAD * 4, bytes_accessed=n * width * 8, transcendentals=heads * n * n
        ),
    )(x)


def per_device(queries, keys, values, query_gain, key_gain):
    tok, width = queries.shape
    half = width // 2
    zl, core = lax.axis_index("zl"), lax.axis_index("c")
    frames = lax.axis_size(FRAME)
    swap = [(0, 1), (1, 0)]

    def shift(a, j):
        return lax.ppermute(a, "zl", [(i, (i + j) % 4) for i in range(4)])

    def column(a, start, size=HEAD):
        return lax.dynamic_slice_in_dim(a, start, size, 1)

    def to_positions(a):
        sent = a.reshape(frames, tok // frames, a.shape[1])
        return lax.all_to_all(sent, FRAME, 0, 0, tiled=True).reshape(a.shape)

    at = jnp.stack([zl, core])
    *parts, keep, sums, three = prep(at, queries, keys, values)
    blocks = [parts[0]] + [shift(parts[j], j) for j in (1, 2, 3)]
    sums = lax.psum(sums, "tp")

    t_sent = norm(three, sums, query_gain[None], key_gain[None])
    stat = jnp.stack([sums[0], sums[4]])
    stats = lax.all_gather(stat, ("zl", "c")).transpose(0, 2, 1).reshape(8 * tok, 2)
    t_sent, blocks, stats = lax.optimization_barrier((t_sent, blocks, stats))
    t_in = to_positions(t_sent)

    swapped = lax.ppermute(pack(blocks, keep), "c", swap)
    outs = spatial(
        at,
        blocks,
        keep,
        swapped,
        stats,
        query_gain[None],
        key_gain[None],
    )
    t_in, last = lax.optimization_barrier((t_in, outs[4]))
    t_out = temporal(t_in, tok // frames)
    t_back = to_positions(t_out)

    moved = [shift(outs[j], 4 - j) for j in (1, 2, 3)]
    moved = lax.optimization_barrier((moved, t_out))[0]
    heads = [outs[0]] + moved
    turned = column(jnp.concatenate(heads + heads[:3], axis=1), (4 - zl) % 4 * HEAD, 4 * HEAD)
    s_half = jnp.concatenate([turned, last], axis=1)
    s_got = lax.ppermute(s_half[tok:], "c", swap)
    s_mine = s_half[:tok]
    s_all = jnp.where(
        core == 0,
        jnp.concatenate([s_mine, s_got], axis=1),
        jnp.concatenate([s_got, s_mine], axis=1),
    )
    return (s_all.astype(jnp.float32) + t_back.astype(jnp.float32)).astype(jnp.bfloat16)


def solution(mesh):
    axes = SEQ + ("tp",)
    split = Mesh(mesh.devices.reshape(4, 2, 2, 4, 2, 4), axes)
    return jax.shard_map(
        per_device,
        mesh=split,
        in_specs=(P(SEQ, "tp"), P(SEQ, "tp"), P(SEQ, "tp"), P("tp"), P("tp")),
        out_specs=P(SEQ, "tp"),
        check_vma=False,
    )
```
